256 devices in a mesh: band: 16 (over x_hi, y, core), dom: 16 (over z, x_lo).
Axes of the slice: x: 4 (x_hi: 2, x_lo: 2; x = x_hi * 2 + x_lo), y: 4, z: 8, core: 2. Of those that a mesh axis runs over, the one named last changes fastest.
Arguments:
- orbitals: float32 [128, 64, 32, 128], P('band', 'dom'), may hold values from -6 to 6
- owner_order: int32 [32], replicated, may hold values from 0 to 31, each once
Outputs:
- exchange_applied: float32 [128, 64, 32, 128], P('band', 'dom')
The draws below stay inside these ranges and needn't reach their ends.
Inputs may be any that keep to these rules, and one draw needn't show every extreme that they name: `owner_order`: a permutation of the block numbers; a block number k names orbitals of the group of index k // 2.
All inputs are finite; a program needn't handle non-finite values.
Results may differ from the reference program's by a relative error of at most 0.0003.
Values sent between devices are 32-bit elements; how exact they have to be, the bound alone decides.
No kernel may reach another device: no remote copies, remote signals or barrier semaphores. Data moves between devices by JAX's collectives and lax.ppermute only.
A program may use at most 192 MiB of HBM per device.

```python
import jax
import jax.numpy as jnp
from jax import lax

LOCAL = 8
BLOCK = 4
STEPS = 2
SWEEPS = 3
NY = 32
NZ = 128
ORBITALS = 128
BLOCKS = 32
NX = 64
N_BAND = 16


def block_scale(stream_key, extent, cuts, least, high):
    gain = 1.0
    for dim, shards_of in cuts:
        heights = jax.random.uniform(jax.random.fold_in(jax.random.fold_in(stream_key, 6), dim), (shards_of,), jnp.float32, least / len(cuts), high / len(cuts))
        gain = gain * jnp.repeat(jnp.exp(heights), extent[dim] // shards_of).reshape((-1,) + (1,) * (len(extent) - 1 - dim))
    return gain


def scatter_about(rng, shape, deviation, most, shards=(), kind=jnp.bfloat16):
    array = deviation * jax.random.normal(rng, shape, jnp.float32)
    if shards:
        array = array * block_scale(rng, shape, shards, -0.22, 0.18)
    return jnp.clip(array, -most, most).astype(kind)


def setup_inputs(seed: int = 0) -> dict:
    streams_of = jax.random.split(jax.random.key(seed), 3)
    orbitals = scatter_about(streams_of[0], (ORBITALS, NX, NY, NZ), 1.0, 6.0, ((0, 16), (1, 16)), jnp.float32)
    owner_order = jax.random.permutation(streams_of[1], BLOCKS).astype(jnp.int32)
    return dict(orbitals=orbitals, owner_order=owner_order)


screen = 0.5
exchange_scale = 0.25


def relax(density):
    potential = density / screen
    for sweep_index in range(SWEEPS):
        neighbours = jnp.roll(potential, -1, 2) + jnp.roll(potential, 1, 2)
        neighbours = neighbours + jnp.roll(potential, -1, 3) + jnp.roll(potential, 1, 3)
        neighbours = neighbours + jnp.roll(potential, -1, 4) + jnp.roll(potential, 1, 4)
        potential = (neighbours + density) / (6.0 + screen)
    return potential


def reference(orbitals, owner_order):
    def group(group_index):
        start = (group_index * LOCAL).astype(jnp.int32)
        local = lax.dynamic_slice_in_dim(orbitals, start, LOCAL, 0)
        applied = jnp.zeros_like(local)
        for step_index in range(STEPS):
            block_id = owner_order[step_index]
            first = (block_id * BLOCK).astype(jnp.int32)
            block = lax.dynamic_slice_in_dim(orbitals, first, BLOCK, 0)
            density = block[:, None] * local[None]
            potential = relax(density)
            applied = applied + jnp.sum(potential * block[:, None], axis=0)
        return -exchange_scale * applied

    result = lax.map(group, jnp.arange(N_BAND, dtype=jnp.int32))
    return result.reshape(orbitals.shape)
```

```python
import itertools

import jax
import jax.numpy as jnp
import numpy as np
from jax import lax
from jax.experimental import pallas as pl
from jax.experimental.pallas import tpu as pltpu
from jax.sharding import PartitionSpec as P

LOCAL = 8
BLOCK = 4
SWEEPS = 3
ROWS = 8
screen = 0.5
exchange_scale = 0.25


def stencil():
    steps = [tuple(s * (d == k) for d in range(3)) for k in range(3) for s in (1, -1)]
    taps = {(0, 0, 0): 1.0 / screen}
    for _ in range(SWEEPS):
        spread = {(0, 0, 0): 1.0}
        for at, weight in taps.items():
            for step in steps:
                to = tuple(a + s for a, s in zip(at, step))
                spread[to] = spread.get(to, 0.0) + weight
        taps = {at: weight / (6.0 + screen) for at, weight in spread.items()}
    return {at: -exchange_scale * weight for at, weight in taps.items()}


TAPS = stencil()
REACH = SWEEPS


def pad_rows(dst, at, layer, cells):
    ny = cells.shape[0]
    dst[at, layer, ROWS : ROWS + ny] = cells
    dst[at, layer, 0:ROWS] = cells[ny - ROWS :]
    dst[at, layer, ROWS + ny :] = cells[:ROWS]


def turned(cells, shift):
    return pltpu.roll(cells, shift % cells.shape[-1], cells.ndim - 1) if shift else cells


def apply_taps(y0, x, pairs, centre, padded_b, padded_phi, sums):
    count = len(sums)
    for reach in range(REACH + 1):
        shifts = (0,) if reach == 0 else (reach, -reach)
        reached = [
            (dx, dy, layer)
            for dx, layer in pairs
            for dy in range(-REACH, REACH + 1)
            if abs(dx) + abs(dy) + reach <= REACH
        ]
        if not reached:
            continue
        here = {dz: [centre(dz, i, x, y0) for i in range(count)] for dz in shifts}
        totals = {dz: [None] * count for dz in shifts}
        for dx, dy, layer in reached:
            rows = pl.ds(y0 + ROWS + dy, ROWS)
            there = [padded_b[i, layer, rows, :] for i in range(count)]
            weights = {}
            for dz in shifts:
                gram = here[dz][0] * there[0]
                for i in range(1, count):
                    gram = gram + here[dz][i] * there[i]
                weights[dz] = gram * np.float32(TAPS[dx, dy, dz])
            for j in range(count):
                phi = padded_phi[j, layer, rows, :]
                for dz in shifts:
                    part = weights[dz] * phi
                    totals[dz][j] = part if totals[dz][j] is None else totals[dz][j] + part
        for dz in shifts:
            for j in range(count):
                sums[j] = sums[j] + turned(totals[dz][j], -dz)
    return sums


def inner_kernel(phi, b_mine, b_other, out, padded_phi, padded_b, rolled):
    count, nx, ny, _ = phi.shape

    def fill(i, _):
        for x in range(nx):
            pad_rows(padded_phi, i, x, phi[i, x])
            pad_rows(padded_phi, i + BLOCK, x, phi[i + BLOCK, x])
            for source, at in ((b_mine, i), (b_other, i + BLOCK)):
                cells = source[i, x]
                pad_rows(padded_b, at, x, cells)
                for dz in range(1, REACH + 1):
                    rolled[2 * dz - 2, at, x] = turned(cells, dz)
                    rolled[2 * dz - 1, at, x] = turned(cells, -dz)
        return 0

    lax.fori_loop(0, BLOCK, fill, 0)

    def centre(dz, i, x, y0):
        if dz == 0:
            return padded_b[i, x, pl.ds(y0 + ROWS, ROWS), :]
        return rolled[2 * abs(dz) - (2 if dz > 0 else 1), i, x, pl.ds(y0, ROWS), :]

    def tile(t, _):
        y0 = pl.multiple_of(t * ROWS, ROWS)
        for x in range(nx):
            pairs = [(to - x, to) for to in range(nx) if abs(to - x) <= REACH]
            sums = [jnp.zeros((ROWS, phi.shape[3]), jnp.float32)] * count
            sums = apply_taps(y0, x, pairs, centre, padded_b, padded_phi, sums)
            for j in range(count):
                out[j, x, pl.ds(y0, ROWS), :] = sums[j]
        return 0

    lax.fori_loop(0, ny // ROWS, tile, 0)


def outer_kernel(
    part, phi_low, phi_high, b_mine, b_other, low_mine, low_other, high_mine, high_other,
    out, padded_phi, padded_b, rolled,
):
    count, nx, ny, _ = part.shape

    def fill(i, _):
        for layer in range(REACH):
            for k in (0, BLOCK):
                pad_rows(padded_phi, i + k, layer, phi_low[i + k, layer])
                pad_rows(padded_phi, i + k, REACH + layer, phi_high[i + k, layer])
            pad_rows(padded_b, i, layer, low_mine[i, layer])
            pad_rows(padded_b, i + BLOCK, layer, low_other[i, layer])
            pad_rows(padded_b, i, REACH + layer, high_mine[i, layer])
            pad_rows(padded_b, i + BLOCK, REACH + layer, high_other[i, layer])
        for x in range(nx):
            for source, at in ((b_mine, i), (b_other, i + BLOCK)):
                cells = source[i, x]
                for dz in range(1, REACH):
                    if dz == 1 or x in (0, nx - 1):
                        rolled[2 * dz - 2, at, x] = turned(cells, dz)
                        rolled[2 * dz - 1, at, x] = turned(cells, -dz)
        return 0

    lax.fori_loop(0, BLOCK, fill, 0)

    def centre(dz, i, x, y0):
        if dz == 0:
            return (b_mine if i < BLOCK else b_other)[i % BLOCK, x, pl.ds(y0, ROWS), :]
        return rolled[2 * abs(dz) - (2 if dz > 0 else 1), i, x, pl.ds(y0, ROWS), :]

    def tile(t, _):
        y0 = pl.multiple_of(t * ROWS, ROWS)
        for x in range(nx):
            pairs = [(layer - REACH - x, layer) for layer in range(REACH) if x - (layer - REACH) <= REACH]
            pairs += [(nx + layer - x, REACH + layer) for layer in range(REACH) if nx + layer - x <= REACH]
            sums = [part[j, x, pl.ds(y0, ROWS), :] for j in range(count)]
            sums = apply_taps(y0, x, pairs, centre, padded_b, padded_phi, sums)
            for j in range(count):
                out[j, x, pl.ds(y0, ROWS), :] = sums[j]
        return 0

    lax.fori_loop(0, ny // ROWS, tile, 0)


def call(kernel, count, nx, ny, nz, layers, rolls, args):
    f32 = jnp.float32
    whole = pl.BlockSpec(memory_space=pltpu.VMEM)
    return pl.pallas_call(
        kernel,
        out_shape=jax.ShapeDtypeStruct((count, nx, ny, nz), f32),
        in_specs=[whole] * len(args),
        out_specs=whole,
        scratch_shapes=[
            pltpu.VMEM((count, layers, ny + 2 * ROWS, nz), f32),
            pltpu.VMEM((count, layers, ny + 2 * ROWS, nz), f32),
            pltpu.VMEM((rolls, count, nx, ny, nz), f32),
        ],
        compiler_params=pltpu.CompilerParams(vmem_limit_bytes=32 * 1024 * 1024),
    )(*args)


def local(orbitals, owner_order):
    count, nx, ny, nz = orbitals.shape
    halves = LOCAL // BLOCK
    band = lax.axis_index("band")
    bands, doms = lax.axis_size("band"), lax.axis_size("dom")
    chips = bands // 2
    core = band % 2
    same_core = [[2 * chip + c for chip in range(chips)] for c in range(2)]
    partner = [(i, i ^ 1) for i in range(bands)]
    up = [(i, (i + 1) % doms) for i in range(doms)]
    down = [((i + 1) % doms, i) for i in range(doms)]

    phi_low = lax.ppermute(orbitals[:, nx - REACH :], "dom", up)
    phi_high = lax.ppermute(orbitals[:, :REACH], "dom", down)

    mine, theirs = owner_order[core], owner_order[1 - core]
    own = lax.dynamic_slice_in_dim(orbitals, mine % halves * BLOCK, BLOCK, 0)
    give = lax.dynamic_slice_in_dim(orbitals, theirs % halves * BLOCK, BLOCK, 0)
    got = lax.ppermute(give, "band", partner)
    owner = mine // halves
    chosen = jnp.where(owner % 2 == core, own, got)
    chunks = chosen.reshape(chips, BLOCK * nx // chips, ny, nz)
    chunks = lax.all_to_all(chunks, "band", 0, 0, axis_index_groups=same_core)
    chunk = lax.dynamic_index_in_dim(chunks, owner // 2, 0, keepdims=True)
    chunks = jnp.broadcast_to(chunk, chunks.shape)
    b_mine = lax.all_to_all(chunks, "band", 0, 0, axis_index_groups=same_core)
    b_mine = b_mine.reshape(BLOCK, nx, ny, nz)

    low_mine = lax.ppermute(b_mine[:, nx - REACH :], "dom", up)
    high_mine = lax.ppermute(b_mine[:, :REACH], "dom", down)
    b_other = lax.ppermute(b_mine, "band", partner)

    part = call(inner_kernel, count, nx, ny, nz, nx, 2 * REACH, (orbitals, b_mine, b_other))

    low_other = lax.ppermute(low_mine, "band", partner)
    high_other = lax.ppermute(high_mine, "band", partner)
    return call(
        outer_kernel, count, nx, ny, nz, 2 * REACH, 2 * REACH - 2,
        (part, phi_low, phi_high, b_mine, b_other, low_mine, low_other, high_mine, high_other),
    )


def solution(mesh):
    in_specs = (P("band", "dom", None, None), P())
    out_specs = P("band", "dom", None, None)
    return jax.shard_map(local, mesh=mesh, in_specs=in_specs, out_specs=out_specs, check_vma=False)
```

```python
import itertools

import jax
import jax.numpy as jnp
import numpy as np
from jax import lax
from jax.experimental import pallas as pl
from jax.experimental.pallas import tpu as pltpu
from jax.sharding import PartitionSpec as P

LOCAL = 8
BLOCK = 4
SWEEPS = 3
ROWS = 8
screen = 0.5
exchange_scale = 0.25


def stencil():
    steps = [tuple(s * (d == k) for d in range(3)) for k in range(3) for s in (1, -1)]
    taps = {(0, 0, 0): 1.0 / screen}
    for _ in range(SWEEPS):
        spread = {(0, 0, 0): 1.0}
        for at, weight in taps.items():
            for step in steps:
                to = tuple(a + s for a, s in zip(at, step))
                spread[to] = spread.get(to, 0.0) + weight
        taps = {at: weight / (6.0 + screen) for at, weight in spread.items()}
    return {at: -exchange_scale * weight for at, weight in taps.items()}


TAPS = stencil()
REACH = SWEEPS


def pad_rows(dst, at, layer, cells):
    ny = cells.shape[0]
    dst[at, layer, ROWS : ROWS + ny] = cells
    dst[at, layer, 0:ROWS] = cells[ny - ROWS :]
    dst[at, layer, ROWS + ny :] = cells[:ROWS]


def turned(cells, shift):
    return pltpu.roll(cells, shift % cells.shape[-1], cells.ndim - 1) if shift else cells


def apply_taps(y0, x, pairs, centre, padded_b, padded_phi, sums):
    count = len(sums)
    for reach in range(REACH + 1):
        shifts = (0,) if reach == 0 else (reach, -reach)
        reached = [
            (dx, dy, layer)
            for dx, layer in pairs
            for dy in range(-REACH, REACH + 1)
            if abs(dx) + abs(dy) + reach <= REACH
        ]
        if not reached:
            continue
        here = {dz: [centre(dz, i, x, y0) for i in range(count)] for dz in shifts}
        totals = {dz: [None] * count for dz in shifts}
        for dx, dy, layer in reached:
            rows = pl.ds(y0 + ROWS + dy, ROWS)
            there = [padded_b[i, layer, rows, :] for i in range(count)]
            weights = {}
            for dz in shifts:
                gram = here[dz][0] * there[0]
                for i in range(1, count):
                    gram = gram + here[dz][i] * there[i]
                weights[dz] = gram * np.float32(TAPS[dx, dy, dz])
            for j in range(count):
                phi = padded_phi[j, layer, rows, :]
                for dz in shifts:
                    part = weights[dz] * phi
                    totals[dz][j] = part if totals[dz][j] is None else totals[dz][j] + part
        for dz in shifts:
            for j in range(count):
                sums[j] = sums[j] + turned(totals[dz][j], -dz)
    return sums


def inner_kernel(phi, b_mine, b_other, out, padded_phi, padded_b, rolled):
    count, nx, ny, _ = phi.shape

    def fill(i, _):
        for x in range(nx):
            pad_rows(padded_phi, i, x, phi[i, x])
            pad_rows(padded_phi, i + BLOCK, x, phi[i + BLOCK, x])
            for source, at in ((b_mine, i), (b_other, i + BLOCK)):
                cells = source[i, x]
                pad_rows(padded_b, at, x, cells)
                for dz in range(1, REACH + 1):
                    rolled[2 * dz - 2, at, x] = turned(cells, dz)
                    rolled[2 * dz - 1, at, x] = turned(cells, -dz)
        return 0

    lax.fori_loop(0, BLOCK, fill, 0)

    def centre(dz, i, x, y0):
        if dz == 0:
            return padded_b[i, x, pl.ds(y0 + ROWS, ROWS), :]
        return rolled[2 * abs(dz) - (2 if dz > 0 else 1), i, x, pl.ds(y0, ROWS), :]

    def tile(t, _):
        y0 = pl.multiple_of(t * ROWS, ROWS)
        for x in range(nx):
            pairs = [(to - x, to) for to in range(nx) if abs(to - x) <= REACH]
            sums = [jnp.zeros((ROWS, phi.shape[3]), jnp.float32)] * count
            sums = apply_taps(y0, x, pairs, centre, padded_b, padded_phi, sums)
            for j in range(count):
                out[j, x, pl.ds(y0, ROWS), :] = sums[j]
        return 0

    lax.fori_loop(0, ny // ROWS, tile, 0)


def outer_kernel(
    part, phi_low, phi_high, b_mine, b_other, low_mine, low_other, high_mine, high_other,
    out, padded_phi, padded_b, rolled,
):
    count, nx, ny, _ = part.shape

    def fill(i, _):
        for layer in range(REACH):
            for k in (0, BLOCK):
                pad_rows(padded_phi, i + k, layer, phi_low[i + k, layer])
                pad_rows(padded_phi, i + k, REACH + layer, phi_high[i + k, layer])
            pad_rows(padded_b, i, layer, low_mine[i, layer])
            pad_rows(padded_b, i + BLOCK, layer, low_other[i, layer])
            pad_rows(padded_b, i, REACH + layer, high_mine[i, layer])
            pad_rows(padded_b, i + BLOCK, REACH + layer, high_other[i, layer])
        for x in range(nx):
            for source, at in ((b_mine, i), (b_other, i + BLOCK)):
                cells = source[i, x]
                for dz in range(1, REACH):
                    if dz == 1 or x in (0, nx - 1):
                        rolled[2 * dz - 2, at, x] = turned(cells, dz)
                        rolled[2 * dz - 1, at, x] = turned(cells, -dz)
        return 0

    lax.fori_loop(0, BLOCK, fill, 0)

    def centre(dz, i, x, y0):
        if dz == 0:
            return (b_mine if i < BLOCK else b_other)[i % BLOCK, x, pl.ds(y0, ROWS), :]
        return rolled[2 * abs(dz) - (2 if dz > 0 else 1), i, x, pl.ds(y0, ROWS), :]

    def tile(t, _):
        y0 = pl.multiple_of(t * ROWS, ROWS)
        for x in range(nx):
            pairs = [(layer - REACH - x, layer) for layer in range(REACH) if x - (layer - REACH) <= REACH]
            pairs += [(nx + layer - x, REACH + layer) for layer in range(REACH) if nx + layer - x <= REACH]
            sums = [part[j, x, pl.ds(y0, ROWS), :] for j in range(count)]
            sums = apply_taps(y0, x, pairs, centre, padded_b, padded_phi, sums)
            for j in range(count):
                out[j, x, pl.ds(y0, ROWS), :] = sums[j]
        return 0

    lax.fori_loop(0, ny // ROWS, tile, 0)


def call(kernel, count, nx, ny, nz, layers, rolls, args):
    f32 = jnp.float32
    whole = pl.BlockSpec(memory_space=pltpu.VMEM)
    return pl.pallas_call(
        kernel,
        out_shape=jax.ShapeDtypeStruct((count, nx, ny, nz), f32),
        in_specs=[whole] * len(args),
        out_specs=whole,
        scratch_shapes=[
            pltpu.VMEM((count, layers, ny + 2 * ROWS, nz), f32),
            pltpu.VMEM((count, layers, ny + 2 * ROWS, nz), f32),
            pltpu.VMEM((rolls, count, nx, ny, nz), f32),
        ],
        compiler_params=pltpu.CompilerParams(vmem_limit_bytes=32 * 1024 * 1024),
    )(*args)


def local(orbitals, owner_order):
    count, nx, ny, nz = orbitals.shape
    halves = LOCAL // BLOCK
    band = lax.axis_index("band")
    bands, doms = lax.axis_size("band"), lax.axis_size("dom")
    chips = bands // 2
    core = band % 2
    same_core = [[2 * chip + c for chip in range(chips)] for c in range(2)]
    partner = [(i, i ^ 1) for i in range(bands)]
    up = [(i, (i + 1) % doms) for i in range(doms)]
    down = [((i + 1) % doms, i) for i in range(doms)]

    phi_low = lax.ppermute(orbitals[:, nx - REACH :], "dom", up)
    phi_high = lax.ppermute(orbitals[:, :REACH], "dom", down)

    got = lax.ppermute(orbitals, "band", partner)
    mine = owner_order[core]
    owner = mine // halves
    chosen = jnp.where(owner % 2 == core, orbitals, got)
    chosen = lax.dynamic_slice_in_dim(chosen, mine % halves * BLOCK, BLOCK, 0)
    chunks = chosen.reshape(chips, BLOCK * nx // chips, ny, nz)
    chunks = lax.all_to_all(chunks, "band", 0, 0, axis_index_groups=same_core)
    chunk = lax.dynamic_index_in_dim(chunks, owner // 2, 0, keepdims=True)
    chunk, phi_low = lax.optimization_barrier((chunk, phi_low))
    chunks = jnp.broadcast_to(chunk, chunks.shape)
    b_mine = lax.all_to_all(chunks, "band", 0, 0, axis_index_groups=same_core)
    b_mine, phi_high = lax.optimization_barrier((b_mine, phi_high))
    b_mine = b_mine.reshape(BLOCK, nx, ny, nz)

    low_mine = lax.ppermute(b_mine[:, nx - REACH :], "dom", up)
    high_mine = lax.ppermute(b_mine[:, :REACH], "dom", down)
    b_other = lax.ppermute(b_mine, "band", partner)
    part = call(inner_kernel, count, nx, ny, nz, nx, 2 * REACH, (orbitals, b_mine, b_other))
    low_mine, high_mine, part = lax.optimization_barrier((low_mine, high_mine, part))

    low_other = lax.ppermute(low_mine, "band", partner)
    high_other = lax.ppermute(high_mine, "band", partner)
    return call(
        outer_kernel, count, nx, ny, nz, 2 * REACH, 2 * REACH - 2,
        (part, phi_low, phi_high, b_mine, b_other, low_mine, low_other, high_mine, high_other),
    )


def solution(mesh):
    in_specs = (P("band", "dom", None, None), P())
    out_specs = P("band", "dom", None, None)
    return jax.shard_map(local, mesh=mesh, in_specs=in_specs, out_specs=out_specs, check_vma=False)
```

```python
import itertools

import jax
import jax.numpy as jnp
import numpy as np
from jax import lax
from jax.experimental import pallas as pl
from jax.experimental.pallas import tpu as pltpu
from jax.sharding import PartitionSpec as P

LOCAL = 8
BLOCK = 4
SWEEPS = 3
ROWS = 8
screen = 0.5
exchange_scale = 0.25


def stencil():
    steps = [tuple(s * (d == k) for d in range(3)) for k in range(3) for s in (1, -1)]
    taps = {(0, 0, 0): 1.0 / screen}
    for _ in range(SWEEPS):
        spread = {(0, 0, 0): 1.0}
        for at, weight in taps.items():
            for step in steps:
                to = tuple(a + s for a, s in zip(at, step))
                spread[to] = spread.get(to, 0.0) + weight
        taps = {at: weight / (6.0 + screen) for at, weight in spread.items()}
    return {at: -exchange_scale * weight for at, weight in taps.items()}


TAPS = stencil()
REACH = SWEEPS


def pad_rows(dst, at, layer, cells):
    ny = cells.shape[0]
    dst[at, layer, ROWS : ROWS + ny] = cells
    dst[at, layer, 0:ROWS] = cells[ny - ROWS :]
    dst[at, layer, ROWS + ny :] = cells[:ROWS]


def turned(cells, shift):
    return pltpu.roll(cells, shift % cells.shape[-1], cells.ndim - 1) if shift else cells


def apply_taps(y0, x, pairs, centre, padded_b, padded_phi, sums):
    count = len(sums)
    for reach in range(REACH + 1):
        shifts = (0,) if reach == 0 else (reach, -reach)
        reached = [
            (dx, dy, layer)
            for dx, layer in pairs
            for dy in range(-REACH, REACH + 1)
            if abs(dx) + abs(dy) + reach <= REACH
        ]
        if not reached:
            continue
        here = {dz: [centre(dz, i, x, y0) for i in range(count)] for dz in shifts}
        totals = {dz: [None] * count for dz in shifts}
        for dx, dy, layer in reached:
            rows = pl.ds(y0 + ROWS + dy, ROWS)
            there = [padded_b[i, layer, rows, :] for i in range(count)]
            weights = {}
            for dz in shifts:
                gram = here[dz][0] * there[0]
                for i in range(1, count):
                    gram = gram + here[dz][i] * there[i]
                weights[dz] = gram * np.float32(TAPS[dx, dy, dz])
            for j in range(count):
                phi = padded_phi[j, layer, rows, :]
                for dz in shifts:
                    part = weights[dz] * phi
                    totals[dz][j] = part if totals[dz][j] is None else totals[dz][j] + part
        for dz in shifts:
            for j in range(count):
                sums[j] = sums[j] + turned(totals[dz][j], -dz)
    return sums


def inner_kernel(phi, b_mine, b_other, out, padded_phi, padded_b, rolled):
    count, nx, ny, _ = phi.shape

    def fill(i, _):
        for x in range(nx):
            pad_rows(padded_phi, i, x, phi[i, x])
            pad_rows(padded_phi, i + BLOCK, x, phi[i + BLOCK, x])
            for source, at in ((b_mine, i), (b_other, i + BLOCK)):
                cells = source[i, x]
                pad_rows(padded_b, at, x, cells)
                for dz in range(1, REACH + 1):
                    rolled[2 * dz - 2, at, x] = turned(cells, dz)
                    rolled[2 * dz - 1, at, x] = turned(cells, -dz)
        return 0

    lax.fori_loop(0, BLOCK, fill, 0)

    def centre(dz, i, x, y0):
        if dz == 0:
            return padded_b[i, x, pl.ds(y0 + ROWS, ROWS), :]
        return rolled[2 * abs(dz) - (2 if dz > 0 else 1), i, x, pl.ds(y0, ROWS), :]

    def tile(t, _):
        y0 = pl.multiple_of(t * ROWS, ROWS)
        for x in range(nx):
            pairs = [(to - x, to) for to in range(nx) if abs(to - x) <= REACH]
            sums = [jnp.zeros((ROWS, phi.shape[3]), jnp.float32)] * count
            sums = apply_taps(y0, x, pairs, centre, padded_b, padded_phi, sums)
            for j in range(count):
                out[j, x, pl.ds(y0, ROWS), :] = sums[j]
        return 0

    lax.fori_loop(0, ny // ROWS, tile, 0)


def outer_kernel(
    part, phi_low, phi_high, b_mine, b_other, low_mine, low_other, high_mine, high_other,
    out, padded_phi, padded_b, rolled,
):
    count, nx, ny, _ = part.shape

    def fill(i, _):
        for layer in range(REACH):
            for k in (0, BLOCK):
                pad_rows(padded_phi, i + k, layer, phi_low[i + k, layer])
                pad_rows(padded_phi, i + k, REACH + layer, phi_high[i + k, layer])
            pad_rows(padded_b, i, layer, low_mine[i, layer])
            pad_rows(padded_b, i + BLOCK, layer, low_other[i, layer])
            pad_rows(padded_b, i, REACH + layer, high_mine[i, layer])
            pad_rows(padded_b, i + BLOCK, REACH + layer, high_other[i, layer])
        for x in range(nx):
            for source, at in ((b_mine, i), (b_other, i + BLOCK)):
                cells = source[i, x]
                for dz in range(1, REACH):
                    if dz == 1 or x in (0, nx - 1):
                        rolled[2 * dz - 2, at, x] = turned(cells, dz)
                        rolled[2 * dz - 1, at, x] = turned(cells, -dz)
        return 0

    lax.fori_loop(0, BLOCK, fill, 0)

    def centre(dz, i, x, y0):
        if dz == 0:
            return (b_mine if i < BLOCK else b_other)[i % BLOCK, x, pl.ds(y0, ROWS), :]
        return rolled[2 * abs(dz) - (2 if dz > 0 else 1), i, x, pl.ds(y0, ROWS), :]

    def tile(t, _):
        y0 = pl.multiple_of(t * ROWS, ROWS)
        for x in range(nx):
            pairs = [(layer - REACH - x, layer) for layer in range(REACH) if x - (layer - REACH) <= REACH]
            pairs += [(nx + layer - x, REACH + layer) for layer in range(REACH) if nx + layer - x <= REACH]
            sums = [part[j, x, pl.ds(y0, ROWS), :] for j in range(count)]
            sums = apply_taps(y0, x, pairs, centre, padded_b, padded_phi, sums)
            for j in range(count):
                out[j, x, pl.ds(y0, ROWS), :] = sums[j]
        return 0

    lax.fori_loop(0, ny // ROWS, tile, 0)


def call(kernel, count, nx, ny, nz, layers, rolls, args):
    f32 = jnp.float32
    whole = pl.BlockSpec(memory_space=pltpu.VMEM)
    return pl.pallas_call(
        kernel,
        out_shape=jax.ShapeDtypeStruct((count, nx, ny, nz), f32),
        in_specs=[whole] * len(args),
        out_specs=whole,
        scratch_shapes=[
            pltpu.VMEM((count, layers, ny + 2 * ROWS, nz), f32),
            pltpu.VMEM((count, layers, ny + 2 * ROWS, nz), f32),
            pltpu.VMEM((rolls, count, nx, ny, nz), f32),
        ],
        compiler_params=pltpu.CompilerParams(vmem_limit_bytes=32 * 1024 * 1024),
    )(*args)


def choose_kernel(order, own, got, chosen, sem):
    core = lax.axis_index("band") & 1
    block = order[core]
    at = (block & 1) * BLOCK

    def copy(source):
        move = pltpu.make_async_copy(source.at[pl.ds(at, BLOCK)], chosen, sem)
        move.start()
        move.wait()

    pl.when((block >> 1) & 1 == core)(lambda: copy(own))
    pl.when((block >> 1) & 1 != core)(lambda: copy(got))


def choose(order, own, got):
    return pl.pallas_call(
        choose_kernel,
        out_shape=jax.ShapeDtypeStruct((BLOCK,) + own.shape[1:], own.dtype),
        in_specs=[
            pl.BlockSpec(memory_space=pltpu.SMEM),
            pl.BlockSpec(memory_space=pl.ANY),
            pl.BlockSpec(memory_space=pl.ANY),
        ],
        out_specs=pl.BlockSpec(memory_space=pltpu.VMEM),
        scratch_shapes=[pltpu.SemaphoreType.DMA],
    )(order, own, got)


def local(orbitals, owner_order):
    count, nx, ny, nz = orbitals.shape
    bands, doms = lax.axis_size("band"), lax.axis_size("dom")
    rows = [[first + 2 * y for y in range(4)] for first in (0, 1, 8, 9)]
    partner = [(i, i ^ 1) for i in range(bands)]
    across = [(i, i ^ 8) for i in range(bands)]
    up = [(i, (i + 1) % doms) for i in range(doms)]
    down = [((i + 1) % doms, i) for i in range(doms)]

    got = lax.ppermute(orbitals, "band", partner)
    chosen = choose(owner_order, orbitals, got)
    chosen, orbitals, owner_order = lax.optimization_barrier((chosen, orbitals, owner_order))

    phi_low = lax.ppermute(orbitals[:, nx - REACH :], "dom", up)
    phi_high = lax.ppermute(orbitals[:, :REACH], "dom", down)

    band = lax.axis_index("band")
    block_id = lax.dynamic_slice_in_dim(owner_order, band & 1, 1)[0]
    chunks = lax.all_to_all(chosen, "band", 0, 0, axis_index_groups=rows, tiled=True)
    chunk = lax.dynamic_slice_in_dim(chunks, (block_id >> 2) & 3, 1, 0)
    chunk, phi_low = lax.optimization_barrier((chunk, phi_low))
    crossed = lax.ppermute(chunk, "band", across)
    chunk = jnp.where(block_id >> 4 == band >> 3, chunk, crossed)
    chunks = jnp.broadcast_to(chunk, chunks.shape)
    b_mine = lax.all_to_all(chunks, "band", 0, 0, axis_index_groups=rows, tiled=True)
    b_mine, phi_high = lax.optimization_barrier((b_mine, phi_high))

    low_mine = lax.ppermute(b_mine[:, nx - REACH :], "dom", up)
    high_mine = lax.ppermute(b_mine[:, :REACH], "dom", down)
    b_other = lax.ppermute(b_mine, "band", partner)
    part = call(inner_kernel, count, nx, ny, nz, nx, 2 * REACH, (orbitals, b_mine, b_other))
    low_mine, high_mine, part = lax.optimization_barrier((low_mine, high_mine, part))

    low_other = lax.ppermute(low_mine, "band", partner)
    high_other = lax.ppermute(high_mine, "band", partner)
    return call(
        outer_kernel, count, nx, ny, nz, 2 * REACH, 2 * REACH - 2,
        (part, phi_low, phi_high, b_mine, b_other, low_mine, low_other, high_mine, high_other),
    )


def solution(mesh):
    in_specs = (P("band", "dom", None, None), P())
    out_specs = P("band", "dom", None, None)
    return jax.shard_map(local, mesh=mesh, in_specs=in_specs, out_specs=out_specs, check_vma=False)
```

```python
import itertools

import jax
import jax.numpy as jnp
import numpy as np
from jax import lax
from jax.experimental import pallas as pl
from jax.experimental.pallas import tpu as pltpu
from jax.sharding import PartitionSpec as P

LOCAL = 8
BLOCK = 4
SWEEPS = 3
ROWS = 8
screen = 0.5
exchange_scale = 0.25


def stencil():
    steps = [tuple(s * (d == k) for d in range(3)) for k in range(3) for s in (1, -1)]
    taps = {(0, 0, 0): 1.0 / screen}
    for _ in range(SWEEPS):
        spread = {(0, 0, 0): 1.0}
        for at, weight in taps.items():
            for step in steps:
                to = tuple(a + s for a, s in zip(at, step))
                spread[to] = spread.get(to, 0.0) + weight
        taps = {at: weight / (6.0 + screen) for at, weight in spread.items()}
    return {at: -exchange_scale * weight for at, weight in taps.items()}


TAPS = stencil()
REACH = SWEEPS


def pad_rows(dst, at, layer, cells):
    ny = cells.shape[0]
    dst[at, layer, ROWS : ROWS + ny] = cells
    dst[at, layer, 0:ROWS] = cells[ny - ROWS :]
    dst[at, layer, ROWS + ny :] = cells[:ROWS]


def turned(cells, shift):
    return pltpu.roll(cells, shift % cells.shape[-1], cells.ndim - 1) if shift else cells


def apply_taps(y0, x, pairs, centre, padded_b, padded_phi, sums):
    count = len(sums)
    for reach in range(REACH + 1):
        shifts = (0,) if reach == 0 else (reach, -reach)
        reached = [
            (dx, dy, layer)
            for dx, layer in pairs
            for dy in range(-REACH, REACH + 1)
            if abs(dx) + abs(dy) + reach <= REACH
        ]
        if not reached:
            continue
        here = {dz: [centre(dz, i, x, y0) for i in range(count)] for dz in shifts}
        totals = {dz: [None] * count for dz in shifts}
        for dx, dy, layer in reached:
            rows = pl.ds(y0 + ROWS + dy, ROWS)
            there = [padded_b[i, layer, rows, :] for i in range(count)]
            weights = {}
            for dz in shifts:
                gram = here[dz][0] * there[0]
                for i in range(1, count):
                    gram = gram + here[dz][i] * there[i]
                weights[dz] = gram * np.float32(TAPS[dx, dy, dz])
            for j in range(count):
                phi = padded_phi[j, layer, rows, :]
                for dz in shifts:
                    part = weights[dz] * phi
                    totals[dz][j] = part if totals[dz][j] is None else totals[dz][j] + part
        for dz in shifts:
            for j in range(count):
                sums[j] = sums[j] + turned(totals[dz][j], -dz)
    return sums


def inner_kernel(phi, b_mine, b_other, out, padded_phi, padded_b, rolled):
    count, nx, ny, _ = phi.shape

    def fill(i, _):
        for x in range(nx):
            pad_rows(padded_phi, i, x, phi[i, x])
            pad_rows(padded_phi, i + BLOCK, x, phi[i + BLOCK, x])
            for source, at in ((b_mine, i), (b_other, i + BLOCK)):
                cells = source[i, x]
                pad_rows(padded_b, at, x, cells)
                for dz in range(1, REACH + 1):
                    rolled[2 * dz - 2, at, x] = turned(cells, dz)
                    rolled[2 * dz - 1, at, x] = turned(cells, -dz)
        return 0

    lax.fori_loop(0, BLOCK, fill, 0)

    def centre(dz, i, x, y0):
        if dz == 0:
            return padded_b[i, x, pl.ds(y0 + ROWS, ROWS), :]
        return rolled[2 * abs(dz) - (2 if dz > 0 else 1), i, x, pl.ds(y0, ROWS), :]

    def tile(t, _):
        y0 = pl.multiple_of(t * ROWS, ROWS)
        for x in range(nx):
            pairs = [(to - x, to) for to in range(nx) if abs(to - x) <= REACH]
            sums = [jnp.zeros((ROWS, phi.shape[3]), jnp.float32)] * count
            sums = apply_taps(y0, x, pairs, centre, padded_b, padded_phi, sums)
            for j in range(count):
                out[j, x, pl.ds(y0, ROWS), :] = sums[j]
        return 0

    lax.fori_loop(0, ny // ROWS, tile, 0)


def outer_kernel(
    part, phi_low, phi_high, b_mine, b_other, low_mine, low_other, high_mine, high_other,
    out, padded_phi, padded_b, rolled,
):
    count, nx, ny, _ = part.shape

    def fill(i, _):
        for layer in range(REACH):
            for k in (0, BLOCK):
                pad_rows(padded_phi, i + k, layer, phi_low[i + k, layer])
                pad_rows(padded_phi, i + k, REACH + layer, phi_high[i + k, layer])
            pad_rows(padded_b, i, layer, low_mine[i, layer])
            pad_rows(padded_b, i + BLOCK, layer, low_other[i, layer])
            pad_rows(padded_b, i, REACH + layer, high_mine[i, layer])
            pad_rows(padded_b, i + BLOCK, REACH + layer, high_other[i, layer])
        for x in range(nx):
            for source, at in ((b_mine, i), (b_other, i + BLOCK)):
                cells = source[i, x]
                for dz in range(1, REACH):
                    if dz == 1 or x in (0, nx - 1):
                        rolled[2 * dz - 2, at, x] = turned(cells, dz)
                        rolled[2 * dz - 1, at, x] = turned(cells, -dz)
        return 0

    lax.fori_loop(0, BLOCK, fill, 0)

    def centre(dz, i, x, y0):
        if dz == 0:
            return (b_mine if i < BLOCK else b_other)[i % BLOCK, x, pl.ds(y0, ROWS), :]
        return rolled[2 * abs(dz) - (2 if dz > 0 else 1), i, x, pl.ds(y0, ROWS), :]

    def tile(t, _):
        y0 = pl.multiple_of(t * ROWS, ROWS)
        for x in range(nx):
            pairs = [(layer - REACH - x, layer) for layer in range(REACH) if x - (layer - REACH) <= REACH]
            pairs += [(nx + layer - x, REACH + layer) for layer in range(REACH) if nx + layer - x <= REACH]
            sums = [part[j, x, pl.ds(y0, ROWS), :] for j in range(count)]
            sums = apply_taps(y0, x, pairs, centre, padded_b, padded_phi, sums)
            for j in range(count):
                out[j, x, pl.ds(y0, ROWS), :] = sums[j]
        return 0

    lax.fori_loop(0, ny // ROWS, tile, 0)


def call(kernel, count, nx, ny, nz, layers, rolls, args):
    f32 = jnp.float32
    whole = pl.BlockSpec(memory_space=pltpu.VMEM)
    return pl.pallas_call(
        kernel,
        out_shape=jax.ShapeDtypeStruct((count, nx, ny, nz), f32),
        in_specs=[whole] * len(args),
        out_specs=whole,
        scratch_shapes=[
            pltpu.VMEM((count, layers, ny + 2 * ROWS, nz), f32),
            pltpu.VMEM((count, layers, ny + 2 * ROWS, nz), f32),
            pltpu.VMEM((rolls, count, nx, ny, nz), f32),
        ],
        compiler_params=pltpu.CompilerParams(vmem_limit_bytes=32 * 1024 * 1024),
    )(*args)


def local(orbitals, owner_order):
    count, nx, ny, nz = orbitals.shape
    bands, doms = lax.axis_size("band"), lax.axis_size("dom")
    partner = [(i, i ^ 1) for i in range(bands)]
    across = [(i, i ^ 8) for i in range(bands)]
    up = [(i, (i + 1) % doms) for i in range(doms)]
    down = [((i + 1) % doms, i) for i in range(doms)]

    def along_y(step):
        return [(i, i // 8 * 8 + (i + 2 * step) % 8) for i in range(bands)]

    pair = lax.ppermute(orbitals, "dom", [(i, i ^ 1) for i in range(doms)])
    onward = [(i, (i + 2 - 4 * (i % 2)) % doms) for i in range(doms)]
    even = lax.axis_index("dom") & 1 == 0

    got = lax.ppermute(orbitals, "band", partner)
    band = lax.axis_index("band")
    core = band & 1
    block_id = jnp.where(core == 0, owner_order[0], owner_order[1])
    here = (block_id >> 1) & 1 == core
    chosen = jnp.where(
        block_id & 1 == 0,
        jnp.where(here, orbitals[:BLOCK], got[:BLOCK]),
        jnp.where(here, orbitals[BLOCK:], got[BLOCK:]),
    )

    below = lax.ppermute(chosen, "band", along_y(1))
    above = lax.ppermute(chosen, "band", along_y(-1))
    opposite = lax.ppermute(chosen, "band", along_y(2))
    ahead = ((block_id >> 2) - (band >> 1)) & 3
    chosen, pair = lax.optimization_barrier((chosen, pair))
    chosen = lax.optimization_barrier(jnp.where(ahead == 0, chosen, 0.0))
    picked = jnp.where(
        ahead < 2, jnp.where(ahead == 0, chosen, above), jnp.where(ahead == 2, opposite, below)
    )
    after, before = pair[:, nx - REACH :], pair[:, :REACH]
    far = lax.ppermute(jnp.where(even, after, before), "dom", onward)
    crossed = lax.ppermute(picked, "band", across)
    picked, far = lax.optimization_barrier((picked, far))
    valid = block_id >> 4 == band >> 3
    picked = lax.optimization_barrier(jnp.where(valid, picked, 0.0))
    b_mine = jnp.where(valid, picked, crossed)

    phi_low = jnp.where(even, far, after)
    phi_high = jnp.where(even, before, far)
    low_mine = lax.ppermute(b_mine[:, nx - REACH :], "dom", up)
    high_mine = lax.ppermute(b_mine[:, :REACH], "dom", down)
    b_other = lax.ppermute(b_mine, "band", partner)
    part = call(inner_kernel, count, nx, ny, nz, nx, 2 * REACH, (orbitals, b_mine, b_other))
    low_mine, high_mine, part, phi_low, phi_high = lax.optimization_barrier(
        (low_mine, high_mine, part, phi_low, phi_high)
    )

    low_other = lax.ppermute(low_mine, "band", partner)
    high_other = lax.ppermute(high_mine, "band", partner)
    return call(
        outer_kernel, count, nx, ny, nz, 2 * REACH, 2 * REACH - 2,
        (part, phi_low, phi_high, b_mine, b_other, low_mine, low_other, high_mine, high_other),
    )


def solution(mesh):
    in_specs = (P("band", "dom", None, None), P())
    out_specs = P("band", "dom", None, None)
    return jax.shard_map(local, mesh=mesh, in_specs=in_specs, out_specs=out_specs, check_vma=False)
```

```python
import itertools

import jax
import jax.numpy as jnp
import numpy as np
from jax import lax
from jax.experimental import pallas as pl
from jax.experimental.pallas import tpu as pltpu
from jax.sharding import PartitionSpec as P

LOCAL = 8
BLOCK = 4
SWEEPS = 3
ROWS = 8
screen = 0.5
exchange_scale = 0.25


def stencil():
    steps = [tuple(s * (d == k) for d in range(3)) for k in range(3) for s in (1, -1)]
    taps = {(0, 0, 0): 1.0 / screen}
    for _ in range(SWEEPS):
        spread = {(0, 0, 0): 1.0}
        for at, weight in taps.items():
            for step in steps:
                to = tuple(a + s for a, s in zip(at, step))
                spread[to] = spread.get(to, 0.0) + weight
        taps = {at: weight / (6.0 + screen) for at, weight in spread.items()}
    return {at: -exchange_scale * weight for at, weight in taps.items()}


TAPS = stencil()
REACH = SWEEPS


def turned(cells, shift):
    return pltpu.roll(cells, shift % cells.shape[-1], cells.ndim - 1) if shift else cells


def apply_taps(x, y0, pairs, sums, centre, b_at, phi_at):
    count = len(sums)
    own = [centre(i, x, y0) for i in range(count)]
    for reach in range(REACH + 1):
        shifts = (0,) if reach == 0 else (reach, -reach)
        reached = [
            (dx, dy, layer)
            for dx, layer in pairs
            for dy in range(-REACH, REACH + 1)
            if abs(dx) + abs(dy) + reach <= REACH
        ]
        if not reached:
            continue
        here = {dz: [turned(cells, dz) for cells in own] for dz in shifts}
        totals = {dz: [None] * count for dz in shifts}
        for dx, dy, layer in reached:
            there = [b_at(i, layer, y0, dy) for i in range(count)]
            weights = {}
            for dz in shifts:
                gram = here[dz][0] * there[0]
                for i in range(1, count):
                    gram = gram + here[dz][i] * there[i]
                weights[dz] = gram * np.float32(TAPS[dx, dy, dz])
            for j in range(count):
                phi = phi_at(j, layer, y0, dy)
                for dz in shifts:
                    part = weights[dz] * phi
                    totals[dz][j] = part if totals[dz][j] is None else totals[dz][j] + part
        for dz in shifts:
            for j in range(count):
                sums[j] = sums[j] + turned(totals[dz][j], -dz)
    return sums


def pad_rows(dst, at, layer, cells):
    ny = cells.shape[0]
    dst[at, layer, ROWS : ROWS + ny] = cells
    dst[at, layer, 0:ROWS] = cells[ny - ROWS :]
    dst[at, layer, ROWS + ny :] = cells[:ROWS]


def inner_kernel(phi, b_mine, b_other, pair, far, out, ends, padded_phi, padded_b):
    count, nx, ny, nz = phi.shape

    def fill(i, _):
        for x in range(nx):
            pad_rows(padded_phi, i, x, phi[i, x])
            pad_rows(padded_phi, i + BLOCK, x, phi[i + BLOCK, x])
            pad_rows(padded_b, i, x, b_mine[i, x])
            pad_rows(padded_b, i + BLOCK, x, b_other[i, x])
        return 0

    lax.fori_loop(0, BLOCK, fill, 0)

    even = lax.axis_index("dom") & 1 == 0

    def fill_ends(low, low_at, high, high_at):
        def fill(i, _):
            for layer in range(REACH):
                pad_rows(ends, i, layer, low[i, low_at + layer])
                pad_rows(ends, i, REACH + layer, high[i, high_at + layer])
            return 0

        lax.fori_loop(0, count, fill, 0)

    pl.when(even)(lambda: fill_ends(far, 0, pair, 0))
    pl.when(jnp.logical_not(even))(lambda: fill_ends(pair, nx - REACH, far, 0))

    def tile(t, _):
        y0 = pl.multiple_of(t * ROWS, ROWS)

        def at(ref):
            return lambda i, layer, y0, dy: ref[i, layer, pl.ds(y0 + ROWS + dy, ROWS), :]

        b_at = at(padded_b)
        for x in range(nx):
            pairs = [(to - x, to) for to in range(nx) if abs(to - x) <= REACH]
            sums = [jnp.zeros((ROWS, nz), jnp.float32)] * count
            sums = apply_taps(
                x, y0, pairs, sums, lambda i, x, y0: b_at(i, x, y0, 0), b_at, at(padded_phi)
            )
            for j in range(count):
                out[j, x, pl.ds(y0, ROWS), :] = sums[j]
        return 0

    lax.fori_loop(0, ny // ROWS, tile, 0)


def outer_kernel(
    part, ends, b_mine, b_other, low_mine, low_other, high_mine, high_other, out, padded_b, done, sems
):
    count, nx, ny, _ = part.shape

    def fill(i, _):
        for layer in range(REACH):
            pad_rows(padded_b, i, layer, low_mine[i, layer])
            pad_rows(padded_b, i + BLOCK, layer, low_other[i, layer])
            pad_rows(padded_b, i, REACH + layer, high_mine[i, layer])
            pad_rows(padded_b, i + BLOCK, REACH + layer, high_other[i, layer])
        return 0

    lax.fori_loop(0, BLOCK, fill, 0)

    def move(y0, t):
        rows = pl.ds(y0, ROWS)
        return pltpu.make_async_copy(done.at[:, :, rows], out.at[:, :, rows], sems.at[t])

    def centre(i, x, y0):
        return (b_mine if i < BLOCK else b_other)[i % BLOCK, x, pl.ds(y0, ROWS), :]

    def tile(t, _):
        y0 = pl.multiple_of(t * ROWS, ROWS)

        def at(ref):
            return lambda i, layer, y0, dy: ref[i, layer, pl.ds(y0 + ROWS + dy, ROWS), :]

        for x in range(nx):
            pairs = [(layer - REACH - x, layer) for layer in range(REACH) if x - (layer - REACH) <= REACH]
            pairs += [(nx + layer - x, REACH + layer) for layer in range(REACH) if nx + layer - x <= REACH]
            sums = [part[j, x, pl.ds(y0, ROWS), :] for j in range(count)]
            sums = apply_taps(x, y0, pairs, sums, centre, at(padded_b), at(ends))
            for j in range(count):
                done[j, x, pl.ds(y0, ROWS), :] = sums[j]
        move(y0, t).start()
        return 0

    lax.fori_loop(0, ny // ROWS, tile, 0)
    for t in range(ny // ROWS):
        move(t * ROWS, t).wait()


def flags_kernel(order, flags):
    band = lax.axis_index("band")
    core = band & 1
    block = order[core]
    rows = (
        block & 1,
        ((block >> 1) & 1) ^ core,
        ((block >> 2) - (band >> 1)) & 3,
        (block >> 4) ^ (band >> 3),
    )
    for row, number in enumerate(rows):
        flags[row : row + 1, :] = jnp.full((1, flags.shape[1]), number, jnp.int32)


def flag_is(flags, row, number, like):
    return jnp.broadcast_to(flags[row : row + 1, :], like.shape) == number


def choose_kernel(flags, own, got, *chosen):
    row = (lax.axis_index("band") >> 1) & 3
    for step, out in enumerate(chosen):
        i = (row + step) & 3
        for x in range(out.shape[0]):
            first, last = own[i, x], own[i + BLOCK, x]
            here = flag_is(flags, 1, 0, first)
            first = jnp.where(here, first, got[i, x])
            last = jnp.where(here, last, got[i + BLOCK, x])
            out[x] = jnp.where(flag_is(flags, 0, 0, first), first, last)


def keep_kernel(cells, kept):
    kept[...] = cells[...]


def pick_kernel(flags, own, above, opposite, below, picked):
    for x in range(picked.shape[0]):
        cells = own[x]
        for number, other in ((1, above), (2, opposite), (3, below)):
            cells = jnp.where(flag_is(flags, 2, number, cells), other[x], cells)
        picked[x] = cells


def settle_kernel(flags, own, crossed, settled):
    for x in range(own.shape[0]):
        cells = own[x]
        settled[x] = jnp.where(flag_is(flags, 3, 0, cells), cells, crossed[x])


def gather_kernel(own, below, opposite, above, block, tail, head):
    nx = own.shape[0]
    for i, source in enumerate((own, below, opposite, above)):
        for x in range(nx):
            cells = source[x]
            block[i, x] = cells
            if x >= nx - REACH:
                tail[i, x - (nx - REACH)] = cells
            if x < REACH:
                head[i, x] = cells


VMEM = pl.BlockSpec(memory_space=pltpu.VMEM)
LIMIT = pltpu.CompilerParams(vmem_limit_bytes=32 * 1024 * 1024)


def call(kernel, shapes, *args, in_specs=None, out_specs=VMEM, scratch=(), kind=jnp.float32):
    shapes = [shapes] if isinstance(shapes[0], int) else list(shapes)
    kinds = kind if isinstance(kind, tuple) else (kind,) * len(shapes)
    outs = [jax.ShapeDtypeStruct(shape, kind) for shape, kind in zip(shapes, kinds)]
    single = len(outs) == 1
    return pl.pallas_call(
        kernel,
        out_shape=outs[0] if single else outs,
        in_specs=in_specs or [VMEM] * len(args),
        out_specs=out_specs if single else [out_specs] * len(outs),
        scratch_shapes=list(scratch),
        compiler_params=LIMIT,
    )(*args)


def local(orbitals, owner_order):
    count, nx, ny, nz = orbitals.shape
    bands, doms = lax.axis_size("band"), lax.axis_size("dom")
    whole, half, side = (count, nx, ny, nz), (BLOCK, nx, ny, nz), (BLOCK, REACH, ny, nz)
    layers = (nx, ny, nz)
    partner = [(i, i ^ 1) for i in range(bands)]
    across = [(i, i ^ 8) for i in range(bands)]
    up = [
        (band * doms + i, (band ^ 8 * (i % 2)) * doms + (i + 1) % doms) for band in range(bands) for i in range(doms)
    ]
    down = [(to, source) for source, to in up]

    def along_y(step):
        return [(i, i // 8 * 8 + (i + 2 * step) % 8) for i in range(bands)]

    pair = lax.ppermute(orbitals, "dom", [(i, i ^ 1) for i in range(doms)])
    onward = [(i, (i + 2 - 4 * (i % 2)) % doms) for i in range(doms)]
    even = lax.axis_index("dom") & 1 == 0

    got = lax.ppermute(orbitals, "band", partner)
    flags = call(
        flags_kernel, (8, nz), owner_order, in_specs=[pl.BlockSpec(memory_space=pltpu.SMEM)], kind=jnp.int32
    )
    chosen = call(choose_kernel, (layers,) * 4, flags, orbitals, got)
    below = lax.ppermute(chosen[1], "band", along_y(1))
    opposite = lax.ppermute(chosen[2], "band", along_y(2))
    above = lax.ppermute(chosen[3], "band", along_y(-1))
    own = chosen[0]
    picked = call(pick_kernel, layers, flags, own, above, opposite, below)
    crossed = lax.ppermute(picked, "band", across)
    picked, pair = lax.optimization_barrier((picked, pair))
    picked = call(keep_kernel, layers, picked)
    settled = call(settle_kernel, layers, flags, picked, crossed)
    far = lax.ppermute(jnp.where(even, pair[:, nx - REACH :], pair[:, :REACH]), "dom", onward)
    below = lax.ppermute(settled, "band", along_y(1))
    opposite = lax.ppermute(settled, "band", along_y(2))
    above = lax.ppermute(settled, "band", along_y(-1))
    b_mine, tail, head = call(gather_kernel, (half, side, side), settled, below, opposite, above)
    low_mine = lax.ppermute(tail, ("band", "dom"), up)
    high_mine = lax.ppermute(head, ("band", "dom"), down)
    b_other = lax.ppermute(b_mine, "band", partner)
    padded = pltpu.VMEM((count, nx, ny + 2 * ROWS, nz), jnp.float32)
    part, ends = call(
        inner_kernel, (whole, (count, 2 * REACH, ny + 2 * ROWS, nz)), orbitals, b_mine, b_other, pair, far,
        scratch=[padded, padded],
    )
    low_mine, high_mine, part = lax.optimization_barrier((low_mine, high_mine, part))

    low_other = lax.ppermute(low_mine, "band", partner)
    high_other = lax.ppermute(high_mine, "band", partner)
    return call(
        outer_kernel, whole, part, ends, b_mine, b_other, low_mine, low_other, high_mine, high_other,
        out_specs=pl.BlockSpec(memory_space=pl.ANY),
        scratch=[
            pltpu.VMEM((count, 2 * REACH, ny + 2 * ROWS, nz), jnp.float32),
            pltpu.VMEM(whole, jnp.float32),
            pltpu.SemaphoreType.DMA((ny // ROWS,)),
        ],
    )


def solution(mesh):
    in_specs = (P("band", "dom", None, None), P())
    out_specs = P("band", "dom", None, None)
    return jax.shard_map(local, mesh=mesh, in_specs=in_specs, out_specs=out_specs, check_vma=False)
```

```python
import itertools

import jax
import jax.numpy as jnp
import numpy as np
from jax import lax
from jax.experimental import pallas as pl
from jax.experimental.pallas import tpu as pltpu
from jax.sharding import PartitionSpec as P

LOCAL = 8
BLOCK = 4
SWEEPS = 3
ROWS = 8
screen = 0.5
exchange_scale = 0.25


def stencil():
    steps = [tuple(s * (d == k) for d in range(3)) for k in range(3) for s in (1, -1)]
    taps = {(0, 0, 0): 1.0 / screen}
    for _ in range(SWEEPS):
        spread = {(0, 0, 0): 1.0}
        for at, weight in taps.items():
            for step in steps:
                to = tuple(a + s for a, s in zip(at, step))
                spread[to] = spread.get(to, 0.0) + weight
        taps = {at: weight / (6.0 + screen) for at, weight in spread.items()}
    return {at: -exchange_scale * weight for at, weight in taps.items()}


TAPS = stencil()
REACH = SWEEPS


def turned(cells, shift):
    return pltpu.roll(cells, shift % cells.shape[-1], cells.ndim - 1) if shift else cells


def apply_taps(x, y0, pairs, sums, centre, b_at, phi_at, weights):
    count = len(sums)
    own = [centre(i, x, y0) for i in range(count)]
    first = x % 2 * (weights.shape[0] // 2)
    plans = []
    for shifts in ((0, 1, -1), (2, -2, 3, -3)):
        plan = []
        here = {}
        for dx, layer in pairs:
            for dy in range(-REACH, REACH + 1):
                slots = {}
                for dz in shifts:
                    if abs(dx) + abs(dy) + abs(dz) <= REACH:
                        slots[dz] = first
                        first += 1
                        if dz not in here:
                            here[dz] = [turned(cells, dz) for cells in own]
                if slots:
                    plan.append((dx, dy, layer, slots))
        plans.append((plan, tuple(here)))
        for dx, dy, layer, slots in plan:
            grams = {}
            for i in range(count):
                there = b_at(i, layer, y0, dy)
                for dz in slots:
                    part = here[dz][i] * there
                    grams[dz] = grams[dz] + part if i else part
            for dz, slot in slots.items():
                weights[slot] = grams[dz] * np.float32(TAPS[dx, dy, dz])
    for plan, shifts in plans:
        totals = {}
        for dx, dy, layer, slots in plan:
            used = {dz: weights[slot] for dz, slot in slots.items()}
            for j in range(count):
                phi = phi_at(j, layer, y0, dy)
                for dz in slots:
                    part = used[dz] * phi
                    totals[dz, j] = totals[dz, j] + part if (dz, j) in totals else part
        for dz in shifts:
            for j in range(count):
                sums[j] = sums[j] + turned(totals[dz, j], -dz)
    return sums


def pad_rows(dst, at, layer, cells):
    ny = cells.shape[0]
    dst[at, layer, ROWS : ROWS + ny] = cells
    dst[at, layer, 0:ROWS] = cells[ny - ROWS :]
    dst[at, layer, ROWS + ny :] = cells[:ROWS]


def inner_kernel(phi, b_mine, b_other, pair, far, out, ends, padded_phi, padded_b, weights):
    count, nx, ny, nz = phi.shape

    def fill(i, _):
        for x in range(nx):
            pad_rows(padded_phi, i, x, phi[i, x])
            pad_rows(padded_phi, i + BLOCK, x, phi[i + BLOCK, x])
            pad_rows(padded_b, i, x, b_mine[i, x])
            pad_rows(padded_b, i + BLOCK, x, b_other[i, x])
        return 0

    lax.fori_loop(0, BLOCK, fill, 0)

    even = lax.axis_index("dom") & 1 == 0

    def fill_ends(low, low_at, high, high_at):
        def fill(i, _):
            for layer in range(REACH):
                pad_rows(ends, i, layer, low[i, low_at + layer])
                pad_rows(ends, i, REACH + layer, high[i, high_at + layer])
            return 0

        lax.fori_loop(0, count, fill, 0)

    pl.when(even)(lambda: fill_ends(far, 0, pair, 0))
    pl.when(jnp.logical_not(even))(lambda: fill_ends(pair, nx - REACH, far, 0))

    def tile(t, _):
        y0 = pl.multiple_of(t * ROWS, ROWS)

        def at(ref):
            return lambda i, layer, y0, dy: ref[i, layer, pl.ds(y0 + ROWS + dy, ROWS), :]

        b_at = at(padded_b)
        for x in range(nx):
            pairs = [(to - x, to) for to in range(nx) if abs(to - x) <= REACH]
            sums = [jnp.zeros((ROWS, nz), jnp.float32)] * count
            sums = apply_taps(
                x, y0, pairs, sums, lambda i, x, y0: b_at(i, x, y0, 0), b_at, at(padded_phi), weights
            )
            for j in range(count):
                out[j, x, pl.ds(y0, ROWS), :] = sums[j]
        return 0

    lax.fori_loop(0, ny // ROWS, tile, 0)


def outer_kernel(
    part, ends, b_mine, b_other, low_mine, low_other, high_mine, high_other,
    out, padded_b, done, weights, sems,
):
    count, nx, ny, _ = part.shape

    def fill(i, _):
        for layer in range(REACH):
            pad_rows(padded_b, i, layer, low_mine[i, layer])
            pad_rows(padded_b, i + BLOCK, layer, low_other[i, layer])
            pad_rows(padded_b, i, REACH + layer, high_mine[i, layer])
            pad_rows(padded_b, i + BLOCK, REACH + layer, high_other[i, layer])
        return 0

    lax.fori_loop(0, BLOCK, fill, 0)

    def move(y0, t):
        rows = pl.ds(y0, ROWS)
        return pltpu.make_async_copy(done.at[:, :, rows], out.at[:, :, rows], sems.at[t])

    def centre(i, x, y0):
        return (b_mine if i < BLOCK else b_other)[i % BLOCK, x, pl.ds(y0, ROWS), :]

    def tile(t, _):
        y0 = pl.multiple_of(t * ROWS, ROWS)

        def at(ref):
            return lambda i, layer, y0, dy: ref[i, layer, pl.ds(y0 + ROWS + dy, ROWS), :]

        for x in range(nx):
            pairs = [(layer - REACH - x, layer) for layer in range(REACH) if x - (layer - REACH) <= REACH]
            pairs += [(nx + layer - x, REACH + layer) for layer in range(REACH) if nx + layer - x <= REACH]
            sums = [part[j, x, pl.ds(y0, ROWS), :] for j in range(count)]
            sums = apply_taps(x, y0, pairs, sums, centre, at(padded_b), at(ends), weights)
            for j in range(count):
                done[j, x, pl.ds(y0, ROWS), :] = sums[j]
        move(y0, t).start()
        return 0

    lax.fori_loop(0, ny // ROWS, tile, 0)
    for t in range(ny // ROWS):
        move(t * ROWS, t).wait()


def flags_kernel(order, flags):
    band = lax.axis_index("band")
    core = band & 1
    block = order[core]
    rows = (
        block & 1,
        ((block >> 1) & 1) ^ core,
        ((block >> 2) ^ (band >> 1)) & 3,
        (block >> 4) ^ (band >> 3),
    )
    for row, number in enumerate(rows):
        flags[row : row + 1, :] = jnp.full((1, flags.shape[1]), number, jnp.int32)


def flag_is(flags, row, number, like):
    return jnp.broadcast_to(flags[row : row + 1, :], like.shape) == number


def choose_kernel(flags, own, got, *chosen):
    row = (lax.axis_index("band") >> 1) & 3
    for step, out in enumerate(chosen):
        i = row ^ step
        for x in range(out.shape[0]):
            first, last = own[i, x], own[i + BLOCK, x]
            here = flag_is(flags, 1, 0, first)
            first = jnp.where(here, first, got[i, x])
            last = jnp.where(here, last, got[i + BLOCK, x])
            out[x] = jnp.where(flag_is(flags, 0, 0, first), first, last)


def keep_kernel(cells, kept):
    kept[...] = cells[...]


def pick_kernel(flags, own, *rest):
    others, picked = rest[:-1], rest[-1]
    for x in range(picked.shape[0]):
        cells = own[x]
        for step, other in enumerate(others, 1):
            cells = jnp.where(flag_is(flags, 2, step, cells), other[x], cells)
        picked[x] = cells


def settle_kernel(flags, own, crossed, settled):
    for x in range(own.shape[0]):
        cells = own[x]
        settled[x] = jnp.where(flag_is(flags, 3, 0, cells), cells, crossed[x])


def gather_kernel(own, first, second, third, block, tail, head):
    nx = own.shape[0]
    for i, source in enumerate((own, first, second, third)):
        for x in range(nx):
            cells = source[x]
            block[i, x] = cells
            if x >= nx - REACH:
                tail[i, x - (nx - REACH)] = cells
            if x < REACH:
                head[i, x] = cells


VMEM = pl.BlockSpec(memory_space=pltpu.VMEM)
LIMIT = pltpu.CompilerParams(vmem_limit_bytes=32 * 1024 * 1024)


def call(kernel, shapes, *args, cost=None, in_specs=None, out_specs=VMEM, scratch=(), kind=jnp.float32):
    shapes = [shapes] if isinstance(shapes[0], int) else list(shapes)
    kinds = kind if isinstance(kind, tuple) else (kind,) * len(shapes)
    outs = [jax.ShapeDtypeStruct(shape, kind) for shape, kind in zip(shapes, kinds)]
    single = len(outs) == 1
    return pl.pallas_call(
        kernel,
        out_shape=outs[0] if single else outs,
        in_specs=in_specs or [VMEM] * len(args),
        out_specs=out_specs if single else [out_specs] * len(outs),
        scratch_shapes=list(scratch),
        compiler_params=LIMIT,
        cost_estimate=cost,
    )(*args)


def local(orbitals, owner_order):
    count, nx, ny, nz = orbitals.shape
    bands, doms = lax.axis_size("band"), lax.axis_size("dom")
    whole, half, side = (count, nx, ny, nz), (BLOCK, nx, ny, nz), (BLOCK, REACH, ny, nz)
    layers = (nx, ny, nz)
    partner = [(i, i ^ 1) for i in range(bands)]
    across = [(i, i ^ 8) for i in range(bands)]
    up = [
        (band * doms + i, (band ^ 8 * (i % 2)) * doms + (i + 1) % doms) for band in range(bands) for i in range(doms)
    ]
    down = [(to, source) for source, to in up]

    def along_y(step):
        return [(i, i ^ 2 * step) for i in range(bands)]

    pair = lax.ppermute(orbitals, "dom", [(i, i ^ 1) for i in range(doms)])
    onward = [(i, (i + 2 - 4 * (i % 2)) % doms) for i in range(doms)]
    even = lax.axis_index("dom") & 1 == 0

    got = lax.ppermute(orbitals, "band", partner)
    flags = call(
        flags_kernel, (8, nz), owner_order, in_specs=[pl.BlockSpec(memory_space=pltpu.SMEM)], kind=jnp.int32,
        cost=pl.CostEstimate(flops=10**9, bytes_accessed=10**7, transcendentals=0),
    )
    chosen = call(choose_kernel, (layers,) * 4, flags, orbitals, got)
    others = [lax.ppermute(chosen[step], "band", along_y(step)) for step in (1, 2, 3)]
    picked = call(pick_kernel, layers, flags, chosen[0], *others)
    crossed = lax.ppermute(picked, "band", across)
    picked, pair = lax.optimization_barrier((picked, pair))
    picked = call(keep_kernel, layers, picked)
    settled = call(settle_kernel, layers, flags, picked, crossed)
    far = lax.ppermute(jnp.where(even, pair[:, nx - REACH :], pair[:, :REACH]), "dom", onward)
    others = [lax.ppermute(settled, "band", along_y(step)) for step in (1, 2, 3)]
    b_mine, tail, head = call(gather_kernel, (half, side, side), settled, *others)

    low_mine = lax.ppermute(tail, ("band", "dom"), up)
    high_mine = lax.ppermute(head, ("band", "dom"), down)
    b_other = lax.ppermute(b_mine, "band", partner)
    padded = pltpu.VMEM((count, nx, ny + 2 * ROWS, nz), jnp.float32)
    weights = pltpu.VMEM((2 * len(TAPS), ROWS, nz), jnp.float32)
    part, ends = call(
        inner_kernel, (whole, (count, 2 * REACH, ny + 2 * ROWS, nz)), orbitals, b_mine, b_other, pair, far,
        scratch=[padded, padded, weights],
    )
    low_mine, high_mine, part = lax.optimization_barrier((low_mine, high_mine, part))

    low_other = lax.ppermute(low_mine, "band", partner)
    high_other = lax.ppermute(high_mine, "band", partner)
    return call(
        outer_kernel, whole, part, ends, b_mine, b_other, low_mine, low_other, high_mine, high_other,
        out_specs=pl.BlockSpec(memory_space=pl.ANY),
        scratch=[
            pltpu.VMEM((count, 2 * REACH, ny + 2 * ROWS, nz), jnp.float32),
            pltpu.VMEM(whole, jnp.float32),
            weights,
            pltpu.SemaphoreType.DMA((ny // ROWS,)),
        ],
    )


def solution(mesh):
    in_specs = (P("band", "dom", None, None), P())
    out_specs = P("band", "dom", None, None)
    return jax.shard_map(local, mesh=mesh, in_specs=in_specs, out_specs=out_specs, check_vma=False)
```
